32 devices in a mesh: groups: 2 (over y), gx: 4 (over z), gy: 4 (over x, core).
Axes of the slice: x: 2, y: 2, z: 4, core: 2. Of those that a mesh axis runs over, the one named last changes fastest.
Arguments:
- tokens: bfloat16 [2048, 8192], P(('groups', 'gy'), 'gx'), parts along dimension 0, may hold values from -70 to 70, as said below
- norm_gain: bfloat16 [8192], P('gx'), may hold values from 0.099609375 to 1.8984375
- w_query: bfloat16 [8192, 4096], P('gx', 'gy'), may hold values from -0.0625 to 0.0625
- w_key: bfloat16 [8192, 1024], P('gx', 'gy'), may hold values from -0.0625 to 0.0625
- w_value: bfloat16 [8192, 1024], P('gx', 'gy'), may hold values from -0.0625 to 0.0625
- w_output: bfloat16 [4096, 8192], P('gy', 'gx'), may hold values from -0.09375 to 0.09375
- sequence_ids: int32 [2048], P('groups'), parts along dimension 0, may hold values from 0 to 3, as said below
Outputs:
- attention_out: bfloat16 [2048, 8192], P(('groups', 'gy'), 'gx'), parts along dimension 0
The draws below stay inside these ranges and needn't reach their ends.
There are 2 independent parts, one for each index of `groups`. The reference program is written for one: setup_inputs(seed, part) draws one part's arguments, and reference() takes and returns one part's arrays. A program takes and returns all parts, laid end to end along the dimension named above; an argument that names none is the same for every part. Nothing has to cross between parts.
Inputs may be any that keep to these rules, and one draw needn't show every extreme that they name: `tokens`: each token's features carry a per-token and a per-feature scale. `sequence_ids`: never falls along the tokens; each id 0 to 3 names one contiguous run of 1 to 512 tokens, one run exactly 512 long.
All inputs are finite; a program needn't handle non-finite values.
Results may differ from the reference program's by a relative error of at most 0.025.
Values may be sent and summed in bfloat16 or wider, within the bound.
A program may use at most 64 MiB of HBM per device.

```python
import jax
import jax.numpy as jnp
from jax import lax

D = 8192
HEADS = 32
KV_HEADS = 8
HEAD_DIM = 128
SEQS = 4
TOKENS = 1024
SEQ_MOST = 512
N_GX = 4
N_GY = 4


def draw_tokens(key, part):
    key = jax.random.fold_in(key, 11)
    key_base, key_rows, key_cols = jax.random.split(key, 3)
    row_scale = 10.0 ** jax.random.uniform(key_rows, (TOKENS, 1), minval=-0.5, maxval=0.5)
    ramp = jnp.arange(D, dtype=jnp.float32)[None, :] / D
    col_noise = 10.0 ** jax.random.uniform(key_cols, (1, D), minval=-0.5, maxval=0.5)
    base = jax.random.truncated_normal(key_base, -4.0, 4.0, (TOKENS, D))
    col_scale = col_noise * 3.0 ** (ramp - 0.5)
    return (base * row_scale * col_scale).astype(jnp.bfloat16)


def draw_sequence_ids(key, part):
    key = jax.random.fold_in(key, 23)
    key_cut, key_long = jax.random.split(key, 2)
    remaining = TOKENS - SEQ_MOST
    order = jax.random.permutation(key_cut, remaining - 1) + 1
    cuts = jnp.sort(order[:SEQS - 2]).astype(jnp.int32)
    edges = jnp.concatenate([jnp.zeros((1,), jnp.int32), cuts, jnp.full((1,), remaining, jnp.int32)])
    short_lengths = edges[1:] - edges[:-1]
    long_slot = jax.random.randint(key_long, (), 0, SEQS)
    slots = jnp.arange(SEQS, dtype=jnp.int32)
    source = jnp.clip(slots - (slots > long_slot).astype(jnp.int32), 0, SEQS - 2)
    lengths = jnp.where(slots == long_slot, jnp.int32(SEQ_MOST), short_lengths[source])
    ends = jnp.cumsum(lengths).astype(jnp.int32)
    token_index = jnp.arange(TOKENS, dtype=jnp.int32)
    ids = jnp.sum((token_index[:, None] >= ends[None, :SEQS - 1]).astype(jnp.int32), axis=1)
    return ids.astype(jnp.int32)


def block_scale(own_key, shape, cuts, least, largest):
    def one(dim, parts):
        steps = jax.random.uniform(jax.random.fold_in(jax.random.fold_in(own_key, 6), dim), (parts,), jnp.float32, least / len(cuts), largest / len(cuts))
        return jnp.repeat(jnp.exp(steps), shape[dim] // parts).reshape((-1,) + (1,) * (len(shape) - dim - 1))

    loudness = one(*cuts[0])
    for cut in cuts[1:]:
        loudness = loudness * one(*cut)
    return loudness


def normal_values(own_key, shape, spread, limit, cuts=(), kind=jnp.bfloat16):
    array = spread * jax.random.normal(own_key, shape, jnp.float32)
    if cuts:
        array = array * block_scale(own_key, shape, cuts, -0.22, 0.18)
    return jnp.clip(array, -limit, limit).astype(kind)


def setup_inputs(seed: int = 0, part: int = 0) -> dict:
    splits = jax.random.split(jax.random.key(seed), 8)
    own_keys = jax.random.split(jax.random.fold_in(splits[7], part), 8)
    return {
        "tokens": draw_tokens(jax.random.fold_in(jax.random.fold_in(splits[7], part), 71), part),
        "norm_gain": jnp.clip(1.0 + 0.18 * jax.random.normal(splits[1], (D,), jnp.float32), 0.099609375, 1.8984375).astype(jnp.bfloat16),
        "w_query": normal_values(splits[2], (D, HEADS * HEAD_DIM), D ** -0.5, 0.0625, ((0, 4), (1, 4))),
        "w_key": normal_values(splits[3], (D, KV_HEADS * HEAD_DIM), D ** -0.5, 0.0625, ((0, 4), (1, 4))),
        "w_value": normal_values(splits[4], (D, KV_HEADS * HEAD_DIM), D ** -0.5, 0.0625, ((0, 4), (1, 4))),
        "w_output": normal_values(splits[5], (HEADS * HEAD_DIM, D), (HEADS * HEAD_DIM) ** -0.5, 0.09375, ((0, 4), (1, 4))),
        "sequence_ids": draw_sequence_ids(jax.random.fold_in(jax.random.fold_in(splits[7], part), 71), part),
    }


norm_epsilon = 1e-05
rope_base = 500000.0

def sequence_positions(sequence_ids):
    length = sequence_ids.shape[0]
    indices = jnp.arange(length, dtype=jnp.int32)
    starts = jnp.concatenate([jnp.ones((1,), jnp.bool_), sequence_ids[1:] != sequence_ids[:-1]])
    first_rows = lax.cummax(jnp.where(starts, indices, jnp.zeros_like(indices)), axis=0)
    return indices - first_rows

def rotate(values, positions):
    row_count = values.shape[0]
    shaped = values.reshape(row_count, -1, HEAD_DIM)
    half_dim = HEAD_DIM // 2
    inverse = rope_base ** (-(jnp.arange(half_dim, dtype=jnp.float32) * 2.0) / HEAD_DIM)
    angles = positions.astype(jnp.float32)[:, None] * inverse[None, :]
    cosine = jnp.cos(angles)[:, None, :]
    sine = jnp.sin(angles)[:, None, :]
    first = shaped[..., :half_dim]
    second = shaped[..., half_dim:]
    turned = jnp.concatenate([first * cosine - second * sine, second * cosine + first * sine], axis=-1)
    return turned.reshape(row_count, -1)

def block_sum(left_side, right_side, blocks):
    block_width = left_side.shape[1] // blocks

    def add_block(running, block_index):
        offset = (block_index * block_width).astype(jnp.int32)
        part = jnp.dot(lax.dynamic_slice_in_dim(left_side, offset, block_width, 1), lax.dynamic_slice_in_dim(right_side, offset, block_width, 0), preferred_element_type=jnp.float32)
        part = lax.optimization_barrier(part.astype(jnp.bfloat16)).astype(jnp.float32)
        return (running + part, None)
    start_value = jnp.zeros((left_side.shape[0], right_side.shape[1]), jnp.float32)
    running, _ = lax.scan(add_block, start_value, jnp.arange(blocks, dtype=jnp.int32))
    return running

def reference(tokens, norm_gain, w_query, w_key, w_value, w_output, sequence_ids):
    wide = tokens.astype(jnp.float32)
    squares = lax.optimization_barrier(jnp.mean(wide * wide, axis=1))
    normed = (wide * lax.rsqrt(squares + norm_epsilon)[:, None] * norm_gain.astype(jnp.float32)[None, :]).astype(jnp.bfloat16)
    positions = sequence_positions(sequence_ids)
    query_raw = block_sum(normed, w_query, N_GX)
    key_raw = block_sum(normed, w_key, N_GX)
    value_raw = block_sum(normed, w_value, N_GX)
    query_rot = rotate(query_raw, positions).astype(jnp.bfloat16)
    key_rot = rotate(key_raw, positions).astype(jnp.bfloat16)
    value_rows = value_raw.astype(jnp.bfloat16)
    length = tokens.shape[0]
    per_group = HEADS // KV_HEADS
    indices = jnp.arange(length, dtype=jnp.int32)
    allowed = (sequence_ids[:, None] == sequence_ids[None, :]) & (indices[None, :] <= indices[:, None])
    query_four = query_rot.reshape(length, KV_HEADS, per_group, HEAD_DIM).transpose(1, 0, 2, 3)
    key_three = key_rot.reshape(length, KV_HEADS, HEAD_DIM).transpose(1, 0, 2)
    value_three = value_rows.reshape(length, KV_HEADS, HEAD_DIM).transpose(1, 0, 2)
    scale = 1.0 / jnp.sqrt(jnp.float32(HEAD_DIM))

    def one_group(operands):
        query_group, key_group, value_group = operands
        scores = jnp.einsum('tqe,pe->tqp', query_group.astype(jnp.float32), key_group.astype(jnp.float32)) * scale
        weights = jnp.where(allowed[:, None, :], jnp.exp(scores), jnp.float32(0.0))
        rounded = lax.optimization_barrier(weights.astype(jnp.bfloat16)).astype(jnp.float32)
        numerator = jnp.einsum('tqp,pe->tqe', rounded, value_group.astype(jnp.float32))
        denominator = lax.optimization_barrier(jnp.sum(weights, axis=-1))
        return numerator / denominator[..., None]
    grouped = lax.map(one_group, (query_four, key_three, value_three))
    attended = grouped.transpose(1, 0, 2, 3).reshape(length, HEADS * HEAD_DIM).astype(jnp.bfloat16)
    return block_sum(attended, w_output, N_GY).astype(jnp.bfloat16)
```

```python
import jax
import jax.numpy as jnp
from jax import lax
from jax.sharding import PartitionSpec as P

D = 8192
HEADS = 32
KV_HEADS = 8
HEAD_DIM = 128


norm_epsilon = 1e-05
rope_base = 500000.0


def sequence_positions(sequence_ids):
    length = sequence_ids.shape[0]
    indices = jnp.arange(length, dtype=jnp.int32)
    starts = jnp.concatenate([jnp.ones((1,), jnp.bool_), sequence_ids[1:] != sequence_ids[:-1]])
    first_rows = lax.cummax(jnp.where(starts, indices, jnp.zeros_like(indices)), axis=0)
    return indices - first_rows


def rotate(values, positions):
    row_count = values.shape[0]
    shaped = values.reshape(row_count, -1, HEAD_DIM)
    half_dim = HEAD_DIM // 2
    inverse = rope_base ** (-(jnp.arange(half_dim, dtype=jnp.float32) * 2.0) / HEAD_DIM)
    angles = positions.astype(jnp.float32)[:, None] * inverse[None, :]
    cosine = jnp.cos(angles)[:, None, :]
    sine = jnp.sin(angles)[:, None, :]
    first = shaped[..., :half_dim]
    second = shaped[..., half_dim:]
    turned = jnp.concatenate(
        [first * cosine - second * sine, second * cosine + first * sine], axis=-1
    )
    return turned.reshape(row_count, -1)


def body(tokens, norm_gain, w_query, w_key, w_value, w_output, sequence_ids):
    length = sequence_ids.shape[0]
    group_size = lax.axis_size("gx")
    row_count = length // group_size
    first_own = lax.axis_index("gx") * row_count
    gain_wide = norm_gain.astype(jnp.float32)[None, :]
    local_rows = tokens.astype(jnp.float32)
    squares = lax.psum(jnp.sum(local_rows * local_rows, axis=1), ("gx",))
    inverse_rms = lax.rsqrt(squares / D + norm_epsilon)
    gained = (local_rows * gain_wide).astype(jnp.bfloat16)
    gathered = lax.all_gather(gained, "gy", axis=0, tiled=True)
    all_rms = lax.all_gather(inverse_rms, "gy", axis=0, tiled=True)
    own_rms = lax.dynamic_slice_in_dim(all_rms, first_own, row_count)
    positions = sequence_positions(sequence_ids)
    own_positions = lax.dynamic_slice_in_dim(positions, first_own, row_count)
    own_ids = lax.dynamic_slice_in_dim(sequence_ids, first_own, row_count)
    own_index = first_own + jnp.arange(row_count, dtype=jnp.int32)
    query_cols = w_query.shape[1]
    kv_cols = w_key.shape[1]
    groups_here = kv_cols // HEAD_DIM
    per_group = HEADS // KV_HEADS
    scale = 1.0 / jnp.sqrt(jnp.float32(HEAD_DIM))
    joined = jnp.concatenate([w_query, w_key, w_value], axis=1)
    summed = lax.psum_scatter(
        jnp.dot(gathered, joined, preferred_element_type=jnp.float32).astype(jnp.bfloat16),
        "gx",
        scatter_dimension=0,
        tiled=True,
    ).astype(jnp.float32) * own_rms[:, None]
    query_rot = rotate(summed[:, :query_cols], own_positions).astype(jnp.bfloat16)
    key_rot = rotate(summed[:, query_cols : query_cols + kv_cols], own_positions).astype(
        jnp.bfloat16
    )
    value_rows = summed[:, query_cols + kv_cols :].astype(jnp.bfloat16)
    query_four = query_rot.reshape(row_count, groups_here, per_group, HEAD_DIM)
    both = lax.all_gather(
        jnp.concatenate([key_rot, value_rows], axis=1), "gx", axis=0, tiled=True
    )
    key_piece = both[:, :kv_cols]
    value_piece = both[:, kv_cols:]
    piece_rows = key_piece.shape[0]
    key_three = key_piece.reshape(piece_rows, groups_here, HEAD_DIM)
    value_three = value_piece.reshape(piece_rows, groups_here, HEAD_DIM)
    scores = (
        jnp.einsum("rgqe,pge->rgqp", query_four, key_three, preferred_element_type=jnp.float32)
        * scale
    )
    key_index = jnp.arange(piece_rows, dtype=jnp.int32)
    allowed = (own_ids[:, None] == sequence_ids[None, :]) & (
        key_index[None, :] <= own_index[:, None]
    )
    weights = jnp.where(allowed[:, None, None, :], jnp.exp(scores), jnp.float32(0.0))
    numerator = jnp.einsum(
        "rgqp,pge->rgqe",
        weights.astype(jnp.bfloat16),
        value_three,
        preferred_element_type=jnp.float32,
    )
    denominator = jnp.sum(weights, axis=-1)
    numerator, denominator = (numerator, denominator)
    attended = (
        (numerator / denominator[..., None]).astype(jnp.bfloat16).reshape(row_count, query_cols)
    )
    partial_value = jnp.dot(
        lax.all_gather(attended, "gx", axis=0, tiled=True),
        w_output,
        preferred_element_type=jnp.float32,
    )
    result = lax.psum_scatter(
        partial_value.astype(jnp.bfloat16), "gy", scatter_dimension=0, tiled=True
    )
    return result


def solution(mesh):
    return jax.shard_map(
        body,
        mesh=mesh,
        in_specs=(
            P(("groups", "gy"), "gx"),
            P("gx"),
            P("gx", "gy"),
            P("gx", "gy"),
            P("gx", "gy"),
            P("gy", "gx"),
            P("groups"),
        ),
        out_specs=P(("groups", "gy"), "gx"),
        check_vma=False,
    )
```

```python
import jax
import jax.numpy as jnp
from jax import lax
from jax.experimental import pallas as pl
from jax.experimental.pallas import tpu as pltpu
from jax.sharding import PartitionSpec as P

D = 8192
HEADS = 32
KV_HEADS = 8
HEAD_DIM = 128


norm_epsilon = 1e-05
rope_base = 500000.0


def sequence_positions(sequence_ids):
    length = sequence_ids.shape[0]
    indices = jnp.arange(length, dtype=jnp.int32)
    starts = jnp.concatenate([jnp.ones((1,), jnp.bool_), sequence_ids[1:] != sequence_ids[:-1]])
    first_rows = lax.cummax(jnp.where(starts, indices, jnp.zeros_like(indices)), axis=0)
    return indices - first_rows


def rotate(values, positions):
    row_count = values.shape[0]
    shaped = values.reshape(row_count, -1, HEAD_DIM)
    half_dim = HEAD_DIM // 2
    inverse = rope_base ** (-(jnp.arange(half_dim, dtype=jnp.float32) * 2.0) / HEAD_DIM)
    angles = positions.astype(jnp.float32)[:, None] * inverse[None, :]
    cosine = jnp.cos(angles)[:, None, :]
    sine = jnp.sin(angles)[:, None, :]
    first = shaped[..., :half_dim]
    second = shaped[..., half_dim:]
    turned = jnp.concatenate(
        [first * cosine - second * sine, second * cosine + first * sine], axis=-1
    )
    return turned.reshape(row_count, -1)


def body(tokens, norm_gain, w_query, w_key, w_value, w_output, sequence_ids):
    length = sequence_ids.shape[0]
    group_size = lax.axis_size("gx")
    row_count = length // group_size
    first_own = lax.axis_index("gx") * row_count
    gain_wide = norm_gain.astype(jnp.float32)[None, :]
    local_rows = tokens.astype(jnp.float32)
    squares = lax.psum(jnp.sum(local_rows * local_rows, axis=1), ("gx",))
    inverse_rms = lax.rsqrt(squares / D + norm_epsilon)
    gained = (local_rows * gain_wide).astype(jnp.bfloat16)
    gathered = lax.all_gather(gained, "gy", axis=0, tiled=True)
    all_rms = lax.all_gather(inverse_rms, "gy", axis=0, tiled=True)
    own_rms = lax.dynamic_slice_in_dim(all_rms, first_own, row_count)
    positions = sequence_positions(sequence_ids)
    own_positions = lax.dynamic_slice_in_dim(positions, first_own, row_count)
    own_ids = lax.dynamic_slice_in_dim(sequence_ids, first_own, row_count)
    own_index = first_own + jnp.arange(row_count, dtype=jnp.int32)
    query_cols = w_query.shape[1]
    kv_cols = w_key.shape[1]
    groups_here = kv_cols // HEAD_DIM
    per_group = HEADS // KV_HEADS
    scale = 1.0 / jnp.sqrt(jnp.float32(HEAD_DIM))
    joined = jnp.concatenate([w_query, w_key, w_value], axis=1)
    summed = lax.psum_scatter(
        jnp.dot(gathered, joined, preferred_element_type=jnp.float32).astype(jnp.bfloat16),
        "gx",
        scatter_dimension=0,
        tiled=True,
    ).astype(jnp.float32) * own_rms[:, None]
    query_rot = rotate(summed[:, :query_cols], own_positions).astype(jnp.bfloat16)
    key_rot = rotate(summed[:, query_cols : query_cols + kv_cols], own_positions).astype(
        jnp.bfloat16
    )
    value_rows = summed[:, query_cols + kv_cols :].astype(jnp.bfloat16)
    query_four = query_rot.reshape(row_count, groups_here, per_group, HEAD_DIM)
    both = lax.all_gather(
        jnp.concatenate([key_rot, value_rows], axis=1), "gx", axis=0, tiled=True
    )
    key_piece = both[:, :kv_cols]
    value_piece = both[:, kv_cols:]
    piece_rows = key_piece.shape[0]
    key_three = key_piece.reshape(piece_rows, groups_here, HEAD_DIM)
    value_three = value_piece.reshape(piece_rows, groups_here, HEAD_DIM)
    scores = (
        jnp.einsum("rgqe,pge->rgqp", query_four, key_three, preferred_element_type=jnp.float32)
        * scale
    )
    key_index = jnp.arange(piece_rows, dtype=jnp.int32)
    allowed = (own_ids[:, None] == sequence_ids[None, :]) & (
        key_index[None, :] <= own_index[:, None]
    )
    weights = jnp.where(allowed[:, None, None, :], jnp.exp(scores), jnp.float32(0.0))
    numerator = jnp.einsum(
        "rgqp,pge->rgqe",
        weights.astype(jnp.bfloat16),
        value_three,
        preferred_element_type=jnp.float32,
    )
    denominator = jnp.sum(weights, axis=-1)
    numerator, denominator = (numerator, denominator)
    attended = (
        (numerator / denominator[..., None]).astype(jnp.bfloat16).reshape(row_count, query_cols)
    )
    partial_value = jnp.dot(
        lax.all_gather(attended, "gx", axis=0, tiled=True),
        w_output,
        preferred_element_type=jnp.float32,
    )
    result = lax.psum_scatter(
        partial_value.astype(jnp.bfloat16), "gy", scatter_dimension=0, tiled=True
    )
    return result


def fused_kernel(
    tokens_ref, gain_ref, wq_ref, wk_ref, wv_ref, wo_ref, cos_ref, sin_ref, idc_ref, idr_ref,
    out_ref,
    xg, ss, ss_in, rms, part, part_in, qs, ks, vs, att, osend, oin,
    x_s, x_r, ss_s, ss_r, r_s, r_r, p_s, p_r, a_s, a_r, o_s, o_r,
):
    rows, feats = tokens_ref.shape
    f32, bf16 = jnp.float32, jnp.bfloat16
    mz = lax.axis_index("gx")
    me = lax.axis_index("gy")
    chip = me // 2
    core_at = me - chip * 2
    core = chip * 2 + 1 - core_at
    across = (1 - chip) * 2 + core_at
    diag = (1 - chip) * 2 + 1 - core_at
    order = [me, core, across, diag]
    z_to = [lax.rem(mz + o, 4) for o in range(4)]
    y_to = [lax.rem(me + o, 4) for o in range(4)]

    barrier = pltpu.get_barrier_semaphore()
    for o in range(1, 4):
        for where in ({"gx": z_to[o]}, {"gy": y_to[o]}):
            pl.semaphore_signal(barrier, inc=1, device_id=where, device_id_type=pl.DeviceIdType.MESH)
    pl.semaphore_wait(barrier, 6)

    def send(src, dst, s, r, where):
        copy = pltpu.make_async_remote_copy(
            src_ref=src, dst_ref=dst, send_sem=s, recv_sem=r,
            device_id=where, device_id_type=pl.DeviceIdType.MESH,
        )
        copy.start()
        return copy

    sent = []
    step = 64

    @pl.loop(0, rows // step)
    def _(i):
        piece = pl.ds(pl.multiple_of(i * step, step), step)
        wide = tokens_ref[piece, :].astype(f32)
        xg[me, piece, :] = (wide * gain_ref[...]).astype(bf16)
        ss[piece, :] = jnp.broadcast_to(jnp.sum(wide * wide, axis=1, keepdims=True), (step, 128))

    to_across = send(xg.at[me], xg.at[me], x_s.at[1], x_r.at[1], {"gy": across})
    to_core = send(xg.at[me], xg.at[me], x_s.at[0], x_r.at[0], {"gy": core})
    ss_copies = [
        send(ss, ss_in.at[o - 1], ss_s.at[o - 1], ss_r.at[o - 1], {"gx": z_to[o]})
        for o in range(1, 4)
    ]
    sent += [to_across, to_core] + ss_copies

    part_copies = []

    def project(j):
        block = order[j]

        @pl.loop(0, 4)
        def _(d):
            cols = pl.ds(pl.multiple_of(d * 256, 256), 256)
            part[j, d, :, 0:256] = jnp.dot(
                xg[block], wq_ref[:, cols], preferred_element_type=f32
            ).astype(bf16)

        for w_ref, at in ((wk_ref, 256), (wv_ref, 384)):
            both = jnp.dot(xg[block], w_ref[...], preferred_element_type=f32).astype(bf16)
            for d in range(4):
                h = d // 2
                part[j, d, :, at : at + 128] = both[:, h * 128 : h * 128 + 128]
        part_copies.append([
            send(part.at[j, z_to[o]], part_in.at[j, o - 1], p_s.at[j, o - 1], p_r.at[j, o - 1],
                 {"gx": z_to[o]})
            for o in (1, 3, 2)
        ])

    project(0)
    to_core.wait_recv()
    project(1)
    for copy in ss_copies:
        copy.wait_recv()
    total = ss[...] + ss_in[0] + ss_in[1] + ss_in[2]
    rms[me] = lax.rsqrt(total / D + norm_epsilon)
    r_copies = [
        send(rms.at[me], rms.at[me], r_s.at[o - 1], r_r.at[o - 1], {"gy": y_to[o]})
        for o in range(1, 4)
    ]
    to_across.wait_recv()
    forward = send(xg.at[across], xg.at[across], x_s.at[2], x_r.at[2], {"gy": core})
    project(2)
    forward.wait_recv()
    project(3)
    sent += [forward] + r_copies
    for copy in r_copies:
        copy.wait_recv()

    for j in range(4):
        for copy in part_copies[j]:
            copy.wait_recv()
        block = order[j]
        here = pl.ds(pl.multiple_of(block * rows, rows), rows)
        scale_rows = rms[block]
        cosine, sine = cos_ref[here, :], sin_ref[here, :]
        for at in range(0, 512, 128):
            cols = slice(at, at + 128)
            value = part[j, mz, :, cols].astype(f32)
            for o in range(3):
                value = value + part_in[j, o, :, cols].astype(f32)
            value = value * scale_rows
            if at < 384:
                value = value * cosine + pltpu.roll(value, 64, 1) * sine
            value = value.astype(bf16)
            if at < 256:
                qs[at // 128, here, :] = value
            elif at == 256:
                ks[here, :] = value
            else:
                vs[here, :] = value
        sent += part_copies[j]

    att_copies = []
    length = ks.shape[0]
    scale = 1.0 / (HEAD_DIM ** 0.5)
    back = [3, 2, 1, 0]
    for j in back:
        block = order[j]
        here = pl.ds(pl.multiple_of(block * rows, rows), rows)
        index_q = block * rows + lax.broadcasted_iota(jnp.int32, (rows, length), 0)
        index_k = lax.broadcasted_iota(jnp.int32, (rows, length), 1)
        allowed = (idc_ref[here, :] == idr_ref[...]) & (index_k <= index_q)
        for h in range(2):
            scores = lax.dot_general(
                qs[h, here, :], ks[...], (((1,), (1,)), ((), ())), preferred_element_type=f32
            ) * scale
            weights = jnp.where(allowed, jnp.exp(scores), 0.0)
            top = jnp.dot(weights.astype(bf16), vs[...], preferred_element_type=f32)
            below = jnp.sum(weights, axis=1, keepdims=True)
            att[j, mz, :, h * 128 : h * 128 + 128] = (top / below).astype(bf16)
        att_copies.append([
            send(att.at[j, mz], att.at[j, mz], a_s.at[j, o - 1], a_r.at[j, o - 1], {"gx": z_to[o]})
            for o in (1, 3, 2)
        ])
    o_copies = {}
    wide_out = wo_ref.shape[1]
    tile = 512
    for n, j in enumerate(back):
        for copy in att_copies[n]:
            copy.wait_recv()
        sent += att_copies[n]
        if j == 2:
            o_copies[3].wait_recv()
        if j == 0:
            o_copies[2].wait_recv()
            o_copies[1].wait_recv()

        @pl.loop(0, wide_out // tile)
        def _(i):
            cols = pl.ds(pl.multiple_of(i * tile, tile), tile)
            value = jnp.dot(att[j, 0], wo_ref[0:256, cols], preferred_element_type=f32)
            for d in range(1, 4):
                value = value + jnp.dot(
                    att[j, d], wo_ref[d * 256 : d * 256 + 256, cols], preferred_element_type=f32
                )
            if j == 2:
                value = value + oin[2, :, cols].astype(f32)
            if j == 0:
                value = value + oin[0, :, cols].astype(f32) + oin[1, :, cols].astype(f32)
                out_ref[:, cols] = value.astype(bf16)
            else:
                osend[j - 1, :, cols] = value.astype(bf16)

        if j > 0:
            o_copies[j] = send(
                osend.at[j - 1], oin.at[j - 1], o_s.at[j - 1], o_r.at[j - 1],
                {"gy": across if j == 2 else core},
            )
            sent.append(o_copies[j])
    for copy in sent:
        copy.wait_send()


def fused_body(tokens, norm_gain, w_query, w_key, w_value, w_output, sequence_ids):
    length = sequence_ids.shape[0]
    rows, feats = tokens.shape
    bf16, f32 = jnp.bfloat16, jnp.float32
    index = jnp.arange(length, dtype=jnp.int32)
    earlier = jnp.sum(
        (sequence_ids[None, :] < sequence_ids[:, None]).astype(jnp.int32), axis=1
    )
    positions = index - earlier
    half = HEAD_DIM // 2
    inverse = rope_base ** (-(jnp.arange(half, dtype=f32) * 2.0) / HEAD_DIM)
    angles = positions.astype(f32)[:, None] * inverse[None, :]
    cosine, sine = jnp.cos(angles), jnp.sin(angles)
    cosine = jnp.concatenate([cosine, cosine], axis=1)
    sine = jnp.concatenate([-sine, sine], axis=1)
    wide_out = w_output.shape[1]
    dma = pltpu.SemaphoreType.DMA
    return pl.pallas_call(
        fused_kernel,
        out_shape=jax.ShapeDtypeStruct((rows, wide_out), bf16),
        in_specs=[pl.BlockSpec(memory_space=pltpu.VMEM)] * 10,
        out_specs=pl.BlockSpec(memory_space=pltpu.VMEM),
        scratch_shapes=[
            pltpu.VMEM((4, rows, feats), bf16),
            pltpu.VMEM((rows, 128), f32),
            pltpu.VMEM((3, rows, 128), f32),
            pltpu.VMEM((4, rows, 128), f32),
            pltpu.VMEM((4, 4, rows, 512), bf16),
            pltpu.VMEM((4, 3, rows, 512), bf16),
            pltpu.VMEM((2, length, 128), bf16),
            pltpu.VMEM((length, 128), bf16),
            pltpu.VMEM((length, 128), bf16),
            pltpu.VMEM((4, 4, rows, 256), bf16),
            pltpu.VMEM((3, rows, wide_out), bf16),
            pltpu.VMEM((3, rows, wide_out), bf16),
            dma((3,)), dma((3,)), dma((3,)), dma((3,)), dma((3,)), dma((3,)),
            dma((4, 3)), dma((4, 3)), dma((4, 3)), dma((4, 3)), dma((3,)), dma((3,)),
        ],
        compiler_params=pltpu.CompilerParams(
            collective_id=0, has_side_effects=True, vmem_limit_bytes=56 * 1024 * 1024
        ),
    )(
        tokens, norm_gain.astype(f32)[None, :], w_query, w_key, w_value, w_output,
        cosine, sine, sequence_ids[:, None], sequence_ids[None, :],
    )


def solution(mesh):
    small = mesh.shape["gx"] == 4 and mesh.shape["gy"] == 4
    return jax.shard_map(
        fused_body if small else body,
        mesh=mesh,
        in_specs=(
            P(("groups", "gy"), "gx"),
            P("gx"),
            P("gx", "gy"),
            P("gx", "gy"),
            P("gx", "gy"),
            P("gy", "gx"),
            P("groups"),
        ),
        out_specs=P(("groups", "gy"), "gx"),
        check_vma=False,
    )
```

```python
import jax
import jax.numpy as jnp
from jax import lax
from jax.experimental import pallas as pl
from jax.experimental.pallas import tpu as pltpu
from jax.sharding import PartitionSpec as P

D = 8192
HEADS = 32
KV_HEADS = 8
HEAD_DIM = 128


norm_epsilon = 1e-05
rope_base = 500000.0


def sequence_positions(sequence_ids):
    length = sequence_ids.shape[0]
    indices = jnp.arange(length, dtype=jnp.int32)
    starts = jnp.concatenate([jnp.ones((1,), jnp.bool_), sequence_ids[1:] != sequence_ids[:-1]])
    first_rows = lax.cummax(jnp.where(starts, indices, jnp.zeros_like(indices)), axis=0)
    return indices - first_rows


def rotate(values, positions):
    row_count = values.shape[0]
    shaped = values.reshape(row_count, -1, HEAD_DIM)
    half_dim = HEAD_DIM // 2
    inverse = rope_base ** (-(jnp.arange(half_dim, dtype=jnp.float32) * 2.0) / HEAD_DIM)
    angles = positions.astype(jnp.float32)[:, None] * inverse[None, :]
    cosine = jnp.cos(angles)[:, None, :]
    sine = jnp.sin(angles)[:, None, :]
    first = shaped[..., :half_dim]
    second = shaped[..., half_dim:]
    turned = jnp.concatenate(
        [first * cosine - second * sine, second * cosine + first * sine], axis=-1
    )
    return turned.reshape(row_count, -1)


def body(tokens, norm_gain, w_query, w_key, w_value, w_output, sequence_ids):
    length = sequence_ids.shape[0]
    group_size = lax.axis_size("gx")
    row_count = length // group_size
    first_own = lax.axis_index("gx") * row_count
    gain_wide = norm_gain.astype(jnp.float32)[None, :]
    local_rows = tokens.astype(jnp.float32)
    squares = lax.psum(jnp.sum(local_rows * local_rows, axis=1), ("gx",))
    inverse_rms = lax.rsqrt(squares / D + norm_epsilon)
    gained = (local_rows * gain_wide).astype(jnp.bfloat16)
    gathered = lax.all_gather(gained, "gy", axis=0, tiled=True)
    all_rms = lax.all_gather(inverse_rms, "gy", axis=0, tiled=True)
    own_rms = lax.dynamic_slice_in_dim(all_rms, first_own, row_count)
    positions = sequence_positions(sequence_ids)
    own_positions = lax.dynamic_slice_in_dim(positions, first_own, row_count)
    own_ids = lax.dynamic_slice_in_dim(sequence_ids, first_own, row_count)
    own_index = first_own + jnp.arange(row_count, dtype=jnp.int32)
    query_cols = w_query.shape[1]
    kv_cols = w_key.shape[1]
    groups_here = kv_cols // HEAD_DIM
    per_group = HEADS // KV_HEADS
    scale = 1.0 / jnp.sqrt(jnp.float32(HEAD_DIM))
    joined = jnp.concatenate([w_query, w_key, w_value], axis=1)
    summed = lax.psum_scatter(
        jnp.dot(gathered, joined, preferred_element_type=jnp.float32).astype(jnp.bfloat16),
        "gx",
        scatter_dimension=0,
        tiled=True,
    ).astype(jnp.float32) * own_rms[:, None]
    query_rot = rotate(summed[:, :query_cols], own_positions).astype(jnp.bfloat16)
    key_rot = rotate(summed[:, query_cols : query_cols + kv_cols], own_positions).astype(
        jnp.bfloat16
    )
    value_rows = summed[:, query_cols + kv_cols :].astype(jnp.bfloat16)
    query_four = query_rot.reshape(row_count, groups_here, per_group, HEAD_DIM)
    both = lax.all_gather(
        jnp.concatenate([key_rot, value_rows], axis=1), "gx", axis=0, tiled=True
    )
    key_piece = both[:, :kv_cols]
    value_piece = both[:, kv_cols:]
    piece_rows = key_piece.shape[0]
    key_three = key_piece.reshape(piece_rows, groups_here, HEAD_DIM)
    value_three = value_piece.reshape(piece_rows, groups_here, HEAD_DIM)
    scores = (
        jnp.einsum("rgqe,pge->rgqp", query_four, key_three, preferred_element_type=jnp.float32)
        * scale
    )
    key_index = jnp.arange(piece_rows, dtype=jnp.int32)
    allowed = (own_ids[:, None] == sequence_ids[None, :]) & (
        key_index[None, :] <= own_index[:, None]
    )
    weights = jnp.where(allowed[:, None, None, :], jnp.exp(scores), jnp.float32(0.0))
    numerator = jnp.einsum(
        "rgqp,pge->rgqe",
        weights.astype(jnp.bfloat16),
        value_three,
        preferred_element_type=jnp.float32,
    )
    denominator = jnp.sum(weights, axis=-1)
    numerator, denominator = (numerator, denominator)
    attended = (
        (numerator / denominator[..., None]).astype(jnp.bfloat16).reshape(row_count, query_cols)
    )
    partial_value = jnp.dot(
        lax.all_gather(attended, "gx", axis=0, tiled=True),
        w_output,
        preferred_element_type=jnp.float32,
    )
    result = lax.psum_scatter(
        partial_value.astype(jnp.bfloat16), "gy", scatter_dimension=0, tiled=True
    )
    return result


def fused_kernel(
    tokens_ref, gain_ref, wq_ref, wk_ref, wv_ref, wo_ref, cos_ref, sin_ref, idc_ref, idr_ref,
    out_ref,
    xg, ss, ss_in, rms, part, part_in, qs, kvs, att, osend, oin,
    x_s, x_r, ss_s, ss_r, r_s, r_r, p_s, p_r, a_s, a_r, o_s, o_r, k_s, k_r,
):
    rows, feats = tokens_ref.shape
    f32, bf16 = jnp.float32, jnp.bfloat16
    mz = lax.axis_index("gx")
    me = lax.axis_index("gy")
    chip = me // 2
    core_at = me - chip * 2
    core = chip * 2 + 1 - core_at
    across = (1 - chip) * 2 + core_at
    diag = (1 - chip) * 2 + 1 - core_at
    order = [me, core, across, diag]
    z_to = [lax.rem(mz + o, 4) for o in range(4)]
    y_to = [lax.rem(me + o, 4) for o in range(4)]

    barrier = pltpu.get_barrier_semaphore()
    for o in range(1, 4):
        for where in ({"gx": z_to[o]}, {"gy": y_to[o]}):
            pl.semaphore_signal(barrier, inc=1, device_id=where, device_id_type=pl.DeviceIdType.MESH)
    pl.semaphore_wait(barrier, 6)

    def send(src, dst, s, r, where):
        copy = pltpu.make_async_remote_copy(
            src_ref=src, dst_ref=dst, send_sem=s, recv_sem=r,
            device_id=where, device_id_type=pl.DeviceIdType.MESH,
        )
        copy.start()
        return copy

    sent = []
    step = 64

    @pl.loop(0, rows // step)
    def _(i):
        piece = pl.ds(pl.multiple_of(i * step, step), step)
        wide = tokens_ref[piece, :].astype(f32)
        xg[me, piece, :] = (wide * gain_ref[...]).astype(bf16)
        ss[piece, :] = jnp.broadcast_to(jnp.sum(wide * wide, axis=1, keepdims=True), (step, 128))

    to_across = send(xg.at[me], xg.at[me], x_s.at[1], x_r.at[1], {"gy": across})
    to_core = send(xg.at[me], xg.at[me], x_s.at[0], x_r.at[0], {"gy": core})
    ss_copies = [
        send(ss, ss_in.at[o - 1], ss_s.at[o - 1], ss_r.at[o - 1], {"gx": z_to[o]})
        for o in range(1, 4)
    ]
    sent += [to_across, to_core] + ss_copies

    sides = [{"gx": lax.rem(mz + 1, 4)}, {"gx": lax.rem(mz + 3, 4)}]
    parity = lax.rem(mz, 2)

    @pl.when(mz == 0)
    def _():
        for j in range(4):
            part_in[j, 0, 0] = jnp.zeros_like(part_in[j, 0, 0])

    @pl.when(mz == 3)
    def _():
        for j in range(4):
            part_in[j, 1, 3] = jnp.zeros_like(part_in[j, 1, 3])

    def part_copy(j, side, d):
        return pltpu.make_async_remote_copy(
            src_ref=part.at[j, d], dst_ref=part_in.at[j, side, d],
            send_sem=p_s.at[j, side, d], recv_sem=p_r.at[j, side, d],
            device_id=sides[side], device_id_type=pl.DeviceIdType.MESH,
        )

    def relay(j):
        for side, d, here in (
            (0, 3, (mz == 1) | (mz == 2)), (1, 0, (mz == 1) | (mz == 2)),
            (0, 2, mz == 1), (1, 1, mz == 2),
        ):
            @pl.when(here)
            def _():
                copy = part_copy(j, side, d)
                copy.wait_recv()
                part[j, d] = (
                    part[j, d].astype(f32) + part_in[j, side, d].astype(f32)
                ).astype(bf16)
                copy.start()

    def project(j):
        block = order[j]

        @pl.loop(0, 4)
        def _(d):
            cols = pl.ds(pl.multiple_of(d * 256, 256), 256)
            part[j, d, :, 0:256] = jnp.dot(
                xg[block], wq_ref[:, cols], preferred_element_type=f32
            ).astype(bf16)

        for w_ref, odd in ((wk_ref, 0), (wv_ref, 1)):
            both = jnp.dot(xg[block], w_ref[...], preferred_element_type=f32).astype(bf16)
            for h in range(2):
                part[j, 2 * h + odd, :, 256:384] = both[:, h * 128 : h * 128 + 128]

        @pl.when(mz == 0)
        def _():
            for d in (3, 2, 1):
                part_copy(j, 0, d).start()

        @pl.when(mz == 3)
        def _():
            for d in (0, 1, 2):
                part_copy(j, 1, d).start()

    project(0)
    to_core.wait_recv()
    project(1)
    for copy in ss_copies:
        copy.wait_recv()
    total = ss[...] + ss_in[0] + ss_in[1] + ss_in[2]
    rms[me] = lax.rsqrt(total / D + norm_epsilon)
    r_copies = [
        send(rms.at[me], rms.at[me], r_s.at[o - 1], r_r.at[o - 1], {"gy": y_to[o]})
        for o in range(1, 4)
    ]
    relay(0)
    to_across.wait_recv()
    forward = send(xg.at[across], xg.at[across], x_s.at[2], x_r.at[2], {"gy": core})
    project(2)
    relay(1)
    forward.wait_recv()
    project(3)
    relay(2)
    sent += [forward] + r_copies
    for copy in r_copies:
        copy.wait_recv()

    kv_copies = []
    for j in range(4):
        if j == 3:
            relay(3)

        @pl.when(mz > 0)
        def _():
            part_copy(j, 0, mz).wait_recv()

        @pl.when(mz < 3)
        def _():
            part_copy(j, 1, mz).wait_recv()

        block = order[j]
        here = pl.ds(pl.multiple_of(block * rows, rows), rows)
        scale_rows = rms[block]
        cosine, sine = cos_ref[here, :], sin_ref[here, :]
        for at in range(0, 384, 128):
            cols = slice(at, at + 128)
            value = (
                part[j, mz, :, cols].astype(f32)
                + part_in[j, 0, mz, :, cols].astype(f32)
                + part_in[j, 1, mz, :, cols].astype(f32)
            ) * scale_rows
            turned = value * cosine + pltpu.roll(value, 64, 1) * sine
            if at < 256:
                qs[at // 128, here, :] = turned.astype(bf16)
            else:
                kvs[parity, here, :] = jnp.where(parity == 0, turned, value).astype(bf16)
        kv_copies.append(send(
            kvs.at[parity, here], kvs.at[parity, here], k_s.at[j], k_r.at[j],
            {"gx": mz + 1 - 2 * parity},
        ))
    for copy in kv_copies:
        copy.wait_recv()
    sent += kv_copies

    length = kvs.shape[1]
    scale = 1.0 / (HEAD_DIM ** 0.5)
    back = [3, 2, 1, 0]

    def att_copy(j, side, source):
        return pltpu.make_async_remote_copy(
            src_ref=att.at[j, source], dst_ref=att.at[j, source],
            send_sem=a_s.at[j, side, source], recv_sem=a_r.at[j, source],
            device_id=sides[side], device_id_type=pl.DeviceIdType.MESH,
        )

    def attend(j):
        block = order[j]
        here = pl.ds(pl.multiple_of(block * rows, rows), rows)
        index_q = block * rows + lax.broadcasted_iota(jnp.int32, (rows, length), 0)
        index_k = lax.broadcasted_iota(jnp.int32, (rows, length), 1)
        allowed = (idc_ref[here, :] == idr_ref[...]) & (index_k <= index_q)
        for h in range(2):
            scores = lax.dot_general(
                qs[h, here, :], kvs[0], (((1,), (1,)), ((), ())), preferred_element_type=f32
            ) * scale
            weights = jnp.where(allowed, jnp.exp(scores), 0.0)
            top = jnp.dot(weights.astype(bf16), kvs[1], preferred_element_type=f32)
            below = jnp.sum(weights, axis=1, keepdims=True)
            att[j, mz, :, h * 128 : h * 128 + 128] = (top / below).astype(bf16)

        @pl.when(mz < 3)
        def _():
            att_copy(j, 0, mz).start()

        @pl.when(mz > 0)
        def _():
            att_copy(j, 1, mz).start()

    def pass_on(j):
        for source in (1, 2, 0, 3):
            @pl.when(mz != source)
            def _():
                att_copy(j, 0, source).wait_recv()

            if source < 2:
                @pl.when((mz > source) & (mz < 3))
                def _():
                    att_copy(j, 0, source).start()
            else:
                @pl.when((mz > 0) & (mz < source))
                def _():
                    att_copy(j, 1, source).start()

    attend(3)
    attend(2)
    attend(1)
    o_copies = {}
    wide_out = wo_ref.shape[1]
    tile = 512
    for n, j in enumerate(back):
        pass_on(j)
        if j == 3:
            attend(0)
        if j == 2:
            o_copies[3].wait_recv()
        if j == 0:
            o_copies[2].wait_recv()
            o_copies[1].wait_recv()

        @pl.loop(0, wide_out // tile)
        def _(i):
            cols = pl.ds(pl.multiple_of(i * tile, tile), tile)
            value = jnp.dot(att[j, 0], wo_ref[0:256, cols], preferred_element_type=f32)
            for d in range(1, 4):
                value = value + jnp.dot(
                    att[j, d], wo_ref[d * 256 : d * 256 + 256, cols], preferred_element_type=f32
                )
            if j == 2:
                value = value + oin[2, :, cols].astype(f32)
            if j == 0:
                value = value + oin[0, :, cols].astype(f32) + oin[1, :, cols].astype(f32)
                out_ref[:, cols] = value.astype(bf16)
            else:
                osend[j - 1, :, cols] = value.astype(bf16)

        if j > 0:
            o_copies[j] = send(
                osend.at[j - 1], oin.at[j - 1], o_s.at[j - 1], o_r.at[j - 1],
                {"gy": across if j == 2 else core},
            )
            sent.append(o_copies[j])
    for copy in sent:
        copy.wait_send()
    for j in range(4):
        for d in range(4):
            if d > 0:
                @pl.when(mz < d)
                def _():
                    part_copy(j, 0, d).wait_send()
            if d < 3:
                @pl.when(mz > d)
                def _():
                    part_copy(j, 1, d).wait_send()

            @pl.when((mz >= d) & (mz < 3))
            def _():
                att_copy(j, 0, d).wait_send()

            @pl.when((mz <= d) & (mz > 0))
            def _():
                att_copy(j, 1, d).wait_send()


def fused_body(tokens, norm_gain, w_query, w_key, w_value, w_output, sequence_ids):
    length = sequence_ids.shape[0]
    rows, feats = tokens.shape
    bf16, f32 = jnp.bfloat16, jnp.float32
    index = jnp.arange(length, dtype=jnp.int32)
    earlier = jnp.sum(
        (sequence_ids[None, :] < sequence_ids[:, None]).astype(jnp.int32), axis=1
    )
    positions = index - earlier
    half = HEAD_DIM // 2
    inverse = rope_base ** (-(jnp.arange(half, dtype=f32) * 2.0) / HEAD_DIM)
    angles = positions.astype(f32)[:, None] * inverse[None, :]
    cosine, sine = jnp.cos(angles), jnp.sin(angles)
    cosine = jnp.concatenate([cosine, cosine], axis=1)
    sine = jnp.concatenate([-sine, sine], axis=1)
    wide_out = w_output.shape[1]
    dma = pltpu.SemaphoreType.DMA
    return pl.pallas_call(
        fused_kernel,
        out_shape=jax.ShapeDtypeStruct((rows, wide_out), bf16),
        in_specs=[pl.BlockSpec(memory_space=pltpu.VMEM)] * 10,
        out_specs=pl.BlockSpec(memory_space=pltpu.VMEM),
        scratch_shapes=[
            pltpu.VMEM((4, rows, feats), bf16),
            pltpu.VMEM((rows, 128), f32),
            pltpu.VMEM((3, rows, 128), f32),
            pltpu.VMEM((4, rows, 128), f32),
            pltpu.VMEM((4, 4, rows, 384), bf16),
            pltpu.VMEM((4, 2, 4, rows, 384), bf16),
            pltpu.VMEM((2, length, 128), bf16),
            pltpu.VMEM((2, length, 128), bf16),
            pltpu.VMEM((4, 4, rows, 256), bf16),
            pltpu.VMEM((3, rows, wide_out), bf16),
            pltpu.VMEM((3, rows, wide_out), bf16),
            dma((3,)), dma((3,)), dma((3,)), dma((3,)), dma((3,)), dma((3,)),
            dma((4, 2, 4)), dma((4, 2, 4)), dma((4, 2, 4)), dma((4, 4)), dma((3,)), dma((3,)),
            dma((4,)), dma((4,)),
        ],
        compiler_params=pltpu.CompilerParams(
            collective_id=0, has_side_effects=True, vmem_limit_bytes=56 * 1024 * 1024
        ),
    )(
        tokens, norm_gain.astype(f32)[None, :], w_query, w_key, w_value, w_output,
        cosine, sine, sequence_ids[:, None], sequence_ids[None, :],
    )


def solution(mesh):
    small = mesh.shape["gx"] == 4 and mesh.shape["gy"] == 4
    return jax.shard_map(
        fused_body if small else body,
        mesh=mesh,
        in_specs=(
            P(("groups", "gy"), "gx"),
            P("gx"),
            P("gx", "gy"),
            P("gx", "gy"),
            P("gx", "gy"),
            P("gy", "gx"),
            P("groups"),
        ),
        out_specs=P(("groups", "gy"), "gx"),
        check_vma=False,
    )
```

```python
import jax
import jax.numpy as jnp
from jax import lax
from jax.experimental import pallas as pl
from jax.experimental.pallas import tpu as pltpu
from jax.sharding import PartitionSpec as P

D = 8192
HEADS = 32
KV_HEADS = 8
HEAD_DIM = 128


norm_epsilon = 1e-05
rope_base = 500000.0


def sequence_positions(sequence_ids):
    length = sequence_ids.shape[0]
    indices = jnp.arange(length, dtype=jnp.int32)
    starts = jnp.concatenate([jnp.ones((1,), jnp.bool_), sequence_ids[1:] != sequence_ids[:-1]])
    first_rows = lax.cummax(jnp.where(starts, indices, jnp.zeros_like(indices)), axis=0)
    return indices - first_rows


def rotate(values, positions):
    row_count = values.shape[0]
    shaped = values.reshape(row_count, -1, HEAD_DIM)
    half_dim = HEAD_DIM // 2
    inverse = rope_base ** (-(jnp.arange(half_dim, dtype=jnp.float32) * 2.0) / HEAD_DIM)
    angles = positions.astype(jnp.float32)[:, None] * inverse[None, :]
    cosine = jnp.cos(angles)[:, None, :]
    sine = jnp.sin(angles)[:, None, :]
    first = shaped[..., :half_dim]
    second = shaped[..., half_dim:]
    turned = jnp.concatenate(
        [first * cosine - second * sine, second * cosine + first * sine], axis=-1
    )
    return turned.reshape(row_count, -1)


def body(tokens, norm_gain, w_query, w_key, w_value, w_output, sequence_ids):
    length = sequence_ids.shape[0]
    group_size = lax.axis_size("gx")
    row_count = length // group_size
    first_own = lax.axis_index("gx") * row_count
    gain_wide = norm_gain.astype(jnp.float32)[None, :]
    local_rows = tokens.astype(jnp.float32)
    squares = lax.psum(jnp.sum(local_rows * local_rows, axis=1), ("gx",))
    inverse_rms = lax.rsqrt(squares / D + norm_epsilon)
    gained = (local_rows * gain_wide).astype(jnp.bfloat16)
    gathered = lax.all_gather(gained, "gy", axis=0, tiled=True)
    all_rms = lax.all_gather(inverse_rms, "gy", axis=0, tiled=True)
    own_rms = lax.dynamic_slice_in_dim(all_rms, first_own, row_count)
    positions = sequence_positions(sequence_ids)
    own_positions = lax.dynamic_slice_in_dim(positions, first_own, row_count)
    own_ids = lax.dynamic_slice_in_dim(sequence_ids, first_own, row_count)
    own_index = first_own + jnp.arange(row_count, dtype=jnp.int32)
    query_cols = w_query.shape[1]
    kv_cols = w_key.shape[1]
    groups_here = kv_cols // HEAD_DIM
    per_group = HEADS // KV_HEADS
    scale = 1.0 / jnp.sqrt(jnp.float32(HEAD_DIM))
    joined = jnp.concatenate([w_query, w_key, w_value], axis=1)
    summed = lax.psum_scatter(
        jnp.dot(gathered, joined, preferred_element_type=jnp.float32).astype(jnp.bfloat16),
        "gx",
        scatter_dimension=0,
        tiled=True,
    ).astype(jnp.float32) * own_rms[:, None]
    query_rot = rotate(summed[:, :query_cols], own_positions).astype(jnp.bfloat16)
    key_rot = rotate(summed[:, query_cols : query_cols + kv_cols], own_positions).astype(
        jnp.bfloat16
    )
    value_rows = summed[:, query_cols + kv_cols :].astype(jnp.bfloat16)
    query_four = query_rot.reshape(row_count, groups_here, per_group, HEAD_DIM)
    both = lax.all_gather(
        jnp.concatenate([key_rot, value_rows], axis=1), "gx", axis=0, tiled=True
    )
    key_piece = both[:, :kv_cols]
    value_piece = both[:, kv_cols:]
    piece_rows = key_piece.shape[0]
    key_three = key_piece.reshape(piece_rows, groups_here, HEAD_DIM)
    value_three = value_piece.reshape(piece_rows, groups_here, HEAD_DIM)
    scores = (
        jnp.einsum("rgqe,pge->rgqp", query_four, key_three, preferred_element_type=jnp.float32)
        * scale
    )
    key_index = jnp.arange(piece_rows, dtype=jnp.int32)
    allowed = (own_ids[:, None] == sequence_ids[None, :]) & (
        key_index[None, :] <= own_index[:, None]
    )
    weights = jnp.where(allowed[:, None, None, :], jnp.exp(scores), jnp.float32(0.0))
    numerator = jnp.einsum(
        "rgqp,pge->rgqe",
        weights.astype(jnp.bfloat16),
        value_three,
        preferred_element_type=jnp.float32,
    )
    denominator = jnp.sum(weights, axis=-1)
    numerator, denominator = (numerator, denominator)
    attended = (
        (numerator / denominator[..., None]).astype(jnp.bfloat16).reshape(row_count, query_cols)
    )
    partial_value = jnp.dot(
        lax.all_gather(attended, "gx", axis=0, tiled=True),
        w_output,
        preferred_element_type=jnp.float32,
    )
    result = lax.psum_scatter(
        partial_value.astype(jnp.bfloat16), "gy", scatter_dimension=0, tiled=True
    )
    return result


def fused_kernel(
    tokens_ref, gain_ref, wq_far, wk_far, wv_far, wo_far, inverse_ref, idr_ref,
    out_ref,
    xg, ss, ss_in, rms, part, part_in, qs, kvs, att, osend, oin,
    x_s, x_r, ss_s, ss_r, r_s, r_r, p_s, p_r, a_s, a_r, o_s, o_r, k_s, k_r,
    wq_ref, wk_ref, wv_ref, wo_ref, w_s, cos_ref, sin_ref, idc_ref,
):
    rows, feats = tokens_ref.shape
    f32, bf16 = jnp.float32, jnp.bfloat16
    mz = lax.axis_index("gx")
    me = lax.axis_index("gy")
    chip = me // 2
    core_at = me - chip * 2
    core = chip * 2 + 1 - core_at
    across = (1 - chip) * 2 + core_at
    diag = (1 - chip) * 2 + 1 - core_at
    order = [me, core, across, diag]
    z_to = [lax.rem(mz + o, 4) for o in range(4)]
    y_to = [lax.rem(me + o, 4) for o in range(4)]

    loads = [
        pltpu.make_async_copy(far, near, w_s.at[i])
        for i, (far, near) in enumerate(
            ((wq_far, wq_ref), (wk_far, wk_ref), (wv_far, wv_ref), (wo_far, wo_ref))
        )
    ]
    for load in loads:
        load.start()
    barrier = pltpu.get_barrier_semaphore()
    for o in range(1, 4):
        for where in ({"gx": z_to[o]}, {"gy": y_to[o]}):
            pl.semaphore_signal(barrier, inc=1, device_id=where, device_id_type=pl.DeviceIdType.MESH)
    pl.semaphore_wait(barrier, 6)

    def send(src, dst, s, r, where):
        copy = pltpu.make_async_remote_copy(
            src_ref=src, dst_ref=dst, send_sem=s, recv_sem=r,
            device_id=where, device_id_type=pl.DeviceIdType.MESH,
        )
        copy.start()
        return copy

    sent = []
    step = 64

    @pl.loop(0, rows // step)
    def _(i):
        piece = pl.ds(pl.multiple_of(i * step, step), step)
        wide = tokens_ref[piece, :].astype(f32)
        xg[me, piece, :] = (wide * gain_ref[...]).astype(bf16)
        ss[piece, :] = jnp.broadcast_to(jnp.sum(wide * wide, axis=1, keepdims=True), (step, 128))

    to_across = send(xg.at[me], xg.at[me], x_s.at[1], x_r.at[1], {"gy": across})
    to_core = send(xg.at[me], xg.at[me], x_s.at[0], x_r.at[0], {"gy": core})
    ss_copies = [
        send(ss, ss_in.at[o - 1], ss_s.at[o - 1], ss_r.at[o - 1], {"gx": z_to[o]})
        for o in range(1, 4)
    ]
    sent += [to_across, to_core] + ss_copies

    sides = [{"gx": lax.rem(mz + 1, 4)}, {"gx": lax.rem(mz + 3, 4)}]
    parity = lax.rem(mz, 2)

    @pl.when(mz == 0)
    def _():
        for j in range(4):
            part_in[j, 0, 0] = jnp.zeros_like(part_in[j, 0, 0])

    @pl.when(mz == 3)
    def _():
        for j in range(4):
            part_in[j, 1, 3] = jnp.zeros_like(part_in[j, 1, 3])

    def part_copy(j, side, d):
        return pltpu.make_async_remote_copy(
            src_ref=part.at[j, d], dst_ref=part_in.at[j, side, d],
            send_sem=p_s.at[j, side, d], recv_sem=p_r.at[j, side, d],
            device_id=sides[side], device_id_type=pl.DeviceIdType.MESH,
        )

    def relay(j):
        for side, d, here in (
            (0, 3, (mz == 1) | (mz == 2)), (1, 0, (mz == 1) | (mz == 2)),
            (0, 2, mz == 1), (1, 1, mz == 2),
        ):
            @pl.when(here)
            def _():
                copy = part_copy(j, side, d)
                copy.wait_recv()
                part[j, d] = (
                    part[j, d].astype(f32) + part_in[j, side, d].astype(f32)
                ).astype(bf16)
                copy.start()

    def project(j):
        block = order[j]

        @pl.loop(0, 4)
        def _(d):
            cols = pl.ds(pl.multiple_of(d * 256, 256), 256)
            part[j, d, :, 0:256] = jnp.dot(
                xg[block], wq_ref[:, cols], preferred_element_type=f32
            ).astype(bf16)

        for w_ref, odd in ((wk_ref, 0), (wv_ref, 1)):
            both = jnp.dot(xg[block], w_ref[...], preferred_element_type=f32).astype(bf16)
            for h in range(2):
                part[j, 2 * h + odd, :, 256:384] = both[:, h * 128 : h * 128 + 128]

        @pl.when(mz == 0)
        def _():
            for d in (3, 2, 1):
                part_copy(j, 0, d).start()

        @pl.when(mz == 3)
        def _():
            for d in (0, 1, 2):
                part_copy(j, 1, d).start()

    for load in loads[:3]:
        load.wait()
    project(0)
    to_core.wait_recv()
    project(1)
    for copy in ss_copies:
        copy.wait_recv()
    total = ss[...] + ss_in[0] + ss_in[1] + ss_in[2]
    rms[me] = lax.rsqrt(total / D + norm_epsilon)
    r_copies = [
        send(rms.at[me], rms.at[me], r_s.at[o - 1], r_r.at[o - 1], {"gy": y_to[o]})
        for o in range(1, 4)
    ]
    relay(0)
    ids_row = idr_ref[...].astype(f32)
    lane = lax.broadcasted_iota(jnp.int32, (128, 128), 1)

    @pl.loop(0, idr_ref.shape[1] // 128)
    def _(i):
        piece = pl.ds(pl.multiple_of(i * 128, 128), 128)
        ids_col = jnp.transpose(
            jnp.broadcast_to(idr_ref[:, piece].astype(f32), (128, 128))
        )
        idc_ref[piece, :] = ids_col
        earlier = jnp.sum(
            jnp.where(ids_row < ids_col[:, 0:1], 1.0, 0.0), axis=1, keepdims=True
        )
        index = i * 128 + lax.broadcasted_iota(jnp.int32, (128, 128), 0)
        angles = (index.astype(f32) - earlier) * inverse_ref[...]
        cos_ref[piece, :] = jnp.cos(angles)
        sine = jnp.sin(angles)
        sin_ref[piece, :] = jnp.where(lane < 64, -sine, sine)

    to_across.wait_recv()
    forward = send(xg.at[across], xg.at[across], x_s.at[2], x_r.at[2], {"gy": core})
    project(2)
    relay(1)
    forward.wait_recv()
    project(3)
    relay(2)
    sent += [forward] + r_copies
    for copy in r_copies:
        copy.wait_recv()

    kv_copies = []
    for j in range(4):
        if j == 3:
            relay(3)

        @pl.when(mz > 0)
        def _():
            part_copy(j, 0, mz).wait_recv()

        @pl.when(mz < 3)
        def _():
            part_copy(j, 1, mz).wait_recv()

        block = order[j]
        here = pl.ds(pl.multiple_of(block * rows, rows), rows)
        scale_rows = rms[block]
        cosine, sine = cos_ref[here, :], sin_ref[here, :]
        for at in range(0, 384, 128):
            cols = slice(at, at + 128)
            value = (
                part[j, mz, :, cols].astype(f32)
                + part_in[j, 0, mz, :, cols].astype(f32)
                + part_in[j, 1, mz, :, cols].astype(f32)
            ) * scale_rows
            turned = value * cosine + pltpu.roll(value, 64, 1) * sine
            if at < 256:
                qs[at // 128, here, :] = turned.astype(bf16)
            else:
                kvs[parity, here, :] = jnp.where(parity == 0, turned, value).astype(bf16)
        kv_copies.append(send(
            kvs.at[parity, here], kvs.at[parity, here], k_s.at[j], k_r.at[j],
            {"gx": mz + 1 - 2 * parity},
        ))
    for copy in kv_copies:
        copy.wait_recv()
    sent += kv_copies

    length = kvs.shape[1]
    scale = 1.0 / (HEAD_DIM ** 0.5)
    back = [3, 2, 1, 0]

    def att_copy(j, side, source):
        return pltpu.make_async_remote_copy(
            src_ref=att.at[j, source], dst_ref=att.at[j, source],
            send_sem=a_s.at[j, side, source], recv_sem=a_r.at[j, source],
            device_id=sides[side], device_id_type=pl.DeviceIdType.MESH,
        )

    def attend(j):
        block = order[j]
        here = pl.ds(pl.multiple_of(block * rows, rows), rows)
        index_q = block * rows + lax.broadcasted_iota(jnp.int32, (rows, length), 0)
        index_k = lax.broadcasted_iota(jnp.int32, (rows, length), 1)
        allowed = (idc_ref[here, 0:1] == ids_row) & (index_k <= index_q)
        for h in range(2):
            scores = lax.dot_general(
                qs[h, here, :], kvs[0], (((1,), (1,)), ((), ())), preferred_element_type=f32
            ) * scale
            weights = jnp.where(allowed, jnp.exp(scores), 0.0)
            top = jnp.dot(weights.astype(bf16), kvs[1], preferred_element_type=f32)
            below = jnp.sum(weights, axis=1, keepdims=True)
            att[j, mz, :, h * 128 : h * 128 + 128] = (top / below).astype(bf16)

        @pl.when(mz < 3)
        def _():
            att_copy(j, 0, mz).start()

        @pl.when(mz > 0)
        def _():
            att_copy(j, 1, mz).start()

    def pass_on(j):
        for source in (1, 2, 0, 3):
            @pl.when(mz != source)
            def _():
                att_copy(j, 0, source).wait_recv()

            if source < 2:
                @pl.when((mz > source) & (mz < 3))
                def _():
                    att_copy(j, 0, source).start()
            else:
                @pl.when((mz > 0) & (mz < source))
                def _():
                    att_copy(j, 1, source).start()

    attend(3)
    attend(2)
    attend(1)
    o_copies = {}
    loads[3].wait()
    wide_out = wo_ref.shape[1]
    tile = 512
    for n, j in enumerate(back):
        pass_on(j)
        if j == 3:
            attend(0)
        if j == 2:
            o_copies[3].wait_recv()
        if j == 0:
            o_copies[2].wait_recv()
            o_copies[1].wait_recv()

        @pl.loop(0, wide_out // tile)
        def _(i):
            cols = pl.ds(pl.multiple_of(i * tile, tile), tile)
            value = jnp.dot(att[j, 0], wo_ref[0:256, cols], preferred_element_type=f32)
            for d in range(1, 4):
                value = value + jnp.dot(
                    att[j, d], wo_ref[d * 256 : d * 256 + 256, cols], preferred_element_type=f32
                )
            if j == 2:
                value = value + oin[2, :, cols].astype(f32)
            if j == 0:
                value = value + oin[0, :, cols].astype(f32) + oin[1, :, cols].astype(f32)
                out_ref[:, cols] = value.astype(bf16)
            else:
                osend[j - 1, :, cols] = value.astype(bf16)

        if j > 0:
            o_copies[j] = send(
                osend.at[j - 1], oin.at[j - 1], o_s.at[j - 1], o_r.at[j - 1],
                {"gy": across if j == 2 else core},
            )
            sent.append(o_copies[j])
    for copy in sent:
        copy.wait_send()
    for j in range(4):
        for d in range(4):
            if d > 0:
                @pl.when(mz < d)
                def _():
                    part_copy(j, 0, d).wait_send()
            if d < 3:
                @pl.when(mz > d)
                def _():
                    part_copy(j, 1, d).wait_send()

            @pl.when((mz >= d) & (mz < 3))
            def _():
                att_copy(j, 0, d).wait_send()

            @pl.when((mz <= d) & (mz > 0))
            def _():
                att_copy(j, 1, d).wait_send()


def fused_body(tokens, norm_gain, w_query, w_key, w_value, w_output, sequence_ids):
    length = sequence_ids.shape[0]
    rows, feats = tokens.shape
    bf16, f32 = jnp.bfloat16, jnp.float32
    half = HEAD_DIM // 2
    inverse = rope_base ** (-(jnp.arange(half, dtype=f32) * 2.0) / HEAD_DIM)
    inverse = jnp.concatenate([inverse, inverse])[None, :]
    wide_out = w_output.shape[1]
    dma = pltpu.SemaphoreType.DMA
    return pl.pallas_call(
        fused_kernel,
        out_shape=jax.ShapeDtypeStruct((rows, wide_out), bf16),
        in_specs=[pl.BlockSpec(memory_space=pltpu.VMEM)] * 2
        + [pl.BlockSpec(memory_space=pl.ANY)] * 4
        + [pl.BlockSpec(memory_space=pltpu.VMEM)] * 2,
        out_specs=pl.BlockSpec(memory_space=pltpu.VMEM),
        scratch_shapes=[
            pltpu.VMEM((4, rows, feats), bf16),
            pltpu.VMEM((rows, 128), f32),
            pltpu.VMEM((3, rows, 128), f32),
            pltpu.VMEM((4, rows, 128), f32),
            pltpu.VMEM((4, 4, rows, 384), bf16),
            pltpu.VMEM((4, 2, 4, rows, 384), bf16),
            pltpu.VMEM((2, length, 128), bf16),
            pltpu.VMEM((2, length, 128), bf16),
            pltpu.VMEM((4, 4, rows, 256), bf16),
            pltpu.VMEM((3, rows, wide_out), bf16),
            pltpu.VMEM((3, rows, wide_out), bf16),
            dma((3,)), dma((3,)), dma((3,)), dma((3,)), dma((3,)), dma((3,)),
            dma((4, 2, 4)), dma((4, 2, 4)), dma((4, 2, 4)), dma((4, 4)), dma((3,)), dma((3,)),
            dma((4,)), dma((4,)),
            pltpu.VMEM(w_query.shape, bf16),
            pltpu.VMEM(w_key.shape, bf16),
            pltpu.VMEM(w_value.shape, bf16),
            pltpu.VMEM(w_output.shape, bf16),
            dma((4,)),
            pltpu.VMEM((length, 128), f32),
            pltpu.VMEM((length, 128), f32),
            pltpu.VMEM((length, 128), f32),
        ],
        compiler_params=pltpu.CompilerParams(
            collective_id=0, has_side_effects=True, vmem_limit_bytes=56 * 1024 * 1024
        ),
    )(
        tokens, norm_gain.astype(f32)[None, :], w_query, w_key, w_value, w_output,
        inverse, sequence_ids[None, :],
    )


def solution(mesh):
    small = mesh.shape["gx"] == 4 and mesh.shape["gy"] == 4
    return jax.shard_map(
        fused_body if small else body,
        mesh=mesh,
        in_specs=(
            P(("groups", "gy"), "gx"),
            P("gx"),
            P("gx", "gy"),
            P("gx", "gy"),
            P("gx", "gy"),
            P("gy", "gx"),
            P("groups"),
        ),
        out_specs=P(("groups", "gy"), "gx"),
        check_vma=False,
    )
```

```python
import jax
import jax.numpy as jnp
from jax import lax
from jax.experimental import pallas as pl
from jax.experimental.pallas import tpu as pltpu
from jax.sharding import PartitionSpec as P

D = 8192
HEADS = 32
KV_HEADS = 8
HEAD_DIM = 128


norm_epsilon = 1e-05
rope_base = 500000.0


def sequence_positions(sequence_ids):
    length = sequence_ids.shape[0]
    indices = jnp.arange(length, dtype=jnp.int32)
    starts = jnp.concatenate([jnp.ones((1,), jnp.bool_), sequence_ids[1:] != sequence_ids[:-1]])
    first_rows = lax.cummax(jnp.where(starts, indices, jnp.zeros_like(indices)), axis=0)
    return indices - first_rows


def rotate(values, positions):
    row_count = values.shape[0]
    shaped = values.reshape(row_count, -1, HEAD_DIM)
    half_dim = HEAD_DIM // 2
    inverse = rope_base ** (-(jnp.arange(half_dim, dtype=jnp.float32) * 2.0) / HEAD_DIM)
    angles = positions.astype(jnp.float32)[:, None] * inverse[None, :]
    cosine = jnp.cos(angles)[:, None, :]
    sine = jnp.sin(angles)[:, None, :]
    first = shaped[..., :half_dim]
    second = shaped[..., half_dim:]
    turned = jnp.concatenate(
        [first * cosine - second * sine, second * cosine + first * sine], axis=-1
    )
    return turned.reshape(row_count, -1)


def body(tokens, norm_gain, w_query, w_key, w_value, w_output, sequence_ids):
    length = sequence_ids.shape[0]
    group_size = lax.axis_size("gx")
    row_count = length // group_size
    first_own = lax.axis_index("gx") * row_count
    gain_wide = norm_gain.astype(jnp.float32)[None, :]
    local_rows = tokens.astype(jnp.float32)
    squares = lax.psum(jnp.sum(local_rows * local_rows, axis=1), ("gx",))
    inverse_rms = lax.rsqrt(squares / D + norm_epsilon)
    gained = (local_rows * gain_wide).astype(jnp.bfloat16)
    gathered = lax.all_gather(gained, "gy", axis=0, tiled=True)
    all_rms = lax.all_gather(inverse_rms, "gy", axis=0, tiled=True)
    own_rms = lax.dynamic_slice_in_dim(all_rms, first_own, row_count)
    positions = sequence_positions(sequence_ids)
    own_positions = lax.dynamic_slice_in_dim(positions, first_own, row_count)
    own_ids = lax.dynamic_slice_in_dim(sequence_ids, first_own, row_count)
    own_index = first_own + jnp.arange(row_count, dtype=jnp.int32)
    query_cols = w_query.shape[1]
    kv_cols = w_key.shape[1]
    groups_here = kv_cols // HEAD_DIM
    per_group = HEADS // KV_HEADS
    scale = 1.0 / jnp.sqrt(jnp.float32(HEAD_DIM))
    joined = jnp.concatenate([w_query, w_key, w_value], axis=1)
    summed = lax.psum_scatter(
        jnp.dot(gathered, joined, preferred_element_type=jnp.float32).astype(jnp.bfloat16),
        "gx",
        scatter_dimension=0,
        tiled=True,
    ).astype(jnp.float32) * own_rms[:, None]
    query_rot = rotate(summed[:, :query_cols], own_positions).astype(jnp.bfloat16)
    key_rot = rotate(summed[:, query_cols : query_cols + kv_cols], own_positions).astype(
        jnp.bfloat16
    )
    value_rows = summed[:, query_cols + kv_cols :].astype(jnp.bfloat16)
    query_four = query_rot.reshape(row_count, groups_here, per_group, HEAD_DIM)
    both = lax.all_gather(
        jnp.concatenate([key_rot, value_rows], axis=1), "gx", axis=0, tiled=True
    )
    key_piece = both[:, :kv_cols]
    value_piece = both[:, kv_cols:]
    piece_rows = key_piece.shape[0]
    key_three = key_piece.reshape(piece_rows, groups_here, HEAD_DIM)
    value_three = value_piece.reshape(piece_rows, groups_here, HEAD_DIM)
    scores = (
        jnp.einsum("rgqe,pge->rgqp", query_four, key_three, preferred_element_type=jnp.float32)
        * scale
    )
    key_index = jnp.arange(piece_rows, dtype=jnp.int32)
    allowed = (own_ids[:, None] == sequence_ids[None, :]) & (
        key_index[None, :] <= own_index[:, None]
    )
    weights = jnp.where(allowed[:, None, None, :], jnp.exp(scores), jnp.float32(0.0))
    numerator = jnp.einsum(
        "rgqp,pge->rgqe",
        weights.astype(jnp.bfloat16),
        value_three,
        preferred_element_type=jnp.float32,
    )
    denominator = jnp.sum(weights, axis=-1)
    numerator, denominator = (numerator, denominator)
    attended = (
        (numerator / denominator[..., None]).astype(jnp.bfloat16).reshape(row_count, query_cols)
    )
    partial_value = jnp.dot(
        lax.all_gather(attended, "gx", axis=0, tiled=True),
        w_output,
        preferred_element_type=jnp.float32,
    )
    result = lax.psum_scatter(
        partial_value.astype(jnp.bfloat16), "gy", scatter_dimension=0, tiled=True
    )
    return result


def fused_kernel(
    tokens_ref, gain_ref, wq_far, wk_far, wv_far, wo_far, inverse_ref, idr_ref,
    out_ref,
    xg, ss, ss_in, rms, part, part_in, qs, kvs, att, osend, oin,
    x_s, x_r, ss_s, ss_r, r_s, r_r, p_s, p_r, a_s, a_r, o_s, o_r, k_s, k_r,
    wq_ref, wk_ref, wv_ref, wo_ref, w_s, cos_ref, sin_ref, idc_ref,
):
    rows, feats = tokens_ref.shape
    f32, bf16 = jnp.float32, jnp.bfloat16
    mz = lax.axis_index("gx")
    me = lax.axis_index("gy")
    chip = me // 2
    core_at = me - chip * 2
    core = chip * 2 + 1 - core_at
    across = (1 - chip) * 2 + core_at
    diag = (1 - chip) * 2 + 1 - core_at
    order = [me, core, across, diag]
    z_to = [lax.rem(mz + o, 4) for o in range(4)]
    y_to = [lax.rem(me + o, 4) for o in range(4)]

    loads = [
        pltpu.make_async_copy(far, near, w_s.at[i])
        for i, (far, near) in enumerate(
            ((wq_far, wq_ref), (wk_far, wk_ref), (wv_far, wv_ref), (wo_far, wo_ref))
        )
    ]
    for load in loads:
        load.start()
    barrier = pltpu.get_barrier_semaphore()
    for o in range(1, 4):
        for where in ({"gx": z_to[o]}, {"gy": y_to[o]}):
            pl.semaphore_signal(barrier, inc=1, device_id=where, device_id_type=pl.DeviceIdType.MESH)
    pl.semaphore_wait(barrier, 6)

    def send(src, dst, s, r, where):
        copy = pltpu.make_async_remote_copy(
            src_ref=src, dst_ref=dst, send_sem=s, recv_sem=r,
            device_id=where, device_id_type=pl.DeviceIdType.MESH,
        )
        copy.start()
        return copy

    sent = []
    step = 64

    @pl.loop(0, rows // step)
    def _(i):
        piece = pl.ds(pl.multiple_of(i * step, step), step)
        wide = tokens_ref[piece, :].astype(f32)
        xg[me, piece, :] = (wide * gain_ref[...].astype(f32)).astype(bf16)
        ss[piece, :] = jnp.broadcast_to(jnp.sum(wide * wide, axis=1, keepdims=True), (step, 128))

    to_across = send(xg.at[me], xg.at[me], x_s.at[1], x_r.at[1], {"gy": across})
    to_core = send(xg.at[me], xg.at[me], x_s.at[0], x_r.at[0], {"gy": core})
    ss_copies = [
        send(ss, ss_in.at[o - 1], ss_s.at[o - 1], ss_r.at[o - 1], {"gx": z_to[o]})
        for o in range(1, 4)
    ]
    sent += [to_across, to_core] + ss_copies

    sides = [{"gx": lax.rem(mz + 1, 4)}, {"gx": lax.rem(mz + 3, 4)}]
    parity = lax.rem(mz, 2)

    @pl.when(mz == 0)
    def _():
        for j in range(4):
            part_in[j, 0, 0] = jnp.zeros_like(part_in[j, 0, 0])

    @pl.when(mz == 3)
    def _():
        for j in range(4):
            part_in[j, 1, 3] = jnp.zeros_like(part_in[j, 1, 3])

    def part_copy(j, side, d):
        return pltpu.make_async_remote_copy(
            src_ref=part.at[j, d], dst_ref=part_in.at[j, side, d],
            send_sem=p_s.at[j, side, d], recv_sem=p_r.at[j, side, d],
            device_id=sides[side], device_id_type=pl.DeviceIdType.MESH,
        )

    def relay(j):
        for side, d, here in (
            (0, 3, (mz == 1) | (mz == 2)), (1, 0, (mz == 1) | (mz == 2)),
            (0, 2, mz == 1), (1, 1, mz == 2),
        ):
            @pl.when(here)
            def _():
                copy = part_copy(j, side, d)
                copy.wait_recv()
                part[j, d] = (
                    part[j, d].astype(f32) + part_in[j, side, d].astype(f32)
                ).astype(bf16)
                copy.start()

    def project(j):
        block = order[j]

        @pl.loop(0, 4)
        def _(d):
            cols = pl.ds(pl.multiple_of(d * 256, 256), 256)
            part[j, d, :, 0:256] = jnp.dot(
                xg[block], wq_ref[:, cols], preferred_element_type=f32
            ).astype(bf16)

        for w_ref, odd in ((wk_ref, 0), (wv_ref, 1)):
            both = jnp.dot(xg[block], w_ref[...], preferred_element_type=f32).astype(bf16)
            for h in range(2):
                part[j, 2 * h + odd, :, 256:384] = both[:, h * 128 : h * 128 + 128]

        @pl.when(mz == 0)
        def _():
            for d in (3, 2, 1):
                part_copy(j, 0, d).start()

        @pl.when(mz == 3)
        def _():
            for d in (0, 1, 2):
                part_copy(j, 1, d).start()

    for load in loads[:3]:
        load.wait()
    project(0)
    to_core.wait_recv()
    project(1)
    for copy in ss_copies:
        copy.wait_recv()
    total = ss[...] + ss_in[0] + ss_in[1] + ss_in[2]
    rms[me] = lax.rsqrt(total / D + norm_epsilon)
    r_copies = [
        send(rms.at[me], rms.at[me], r_s.at[o - 1], r_r.at[o - 1], {"gy": y_to[o]})
        for o in range(1, 4)
    ]
    relay(0)
    ids_row = idr_ref[...].astype(f32)
    lane = lax.broadcasted_iota(jnp.int32, (128, 128), 1)

    @pl.loop(0, idr_ref.shape[1] // 128)
    def _(i):
        piece = pl.ds(pl.multiple_of(i * 128, 128), 128)
        ids_col = jnp.transpose(
            jnp.broadcast_to(idr_ref[:, piece].astype(f32), (128, 128))
        )
        idc_ref[piece, :] = ids_col
        earlier = jnp.sum(
            jnp.where(ids_row < ids_col[:, 0:1], 1.0, 0.0), axis=1, keepdims=True
        )
        index = i * 128 + lax.broadcasted_iota(jnp.int32, (128, 128), 0)
        angles = (index.astype(f32) - earlier) * inverse_ref[...]
        cos_ref[piece, :] = jnp.cos(angles)
        sine = jnp.sin(angles)
        sin_ref[piece, :] = jnp.where(lane < 64, -sine, sine)

    relay(1)
    to_across.wait_recv()
    forward = send(xg.at[across], xg.at[across], x_s.at[2], x_r.at[2], {"gy": core})
    project(2)
    forward.wait_recv()
    project(3)
    relay(2)
    sent += [forward] + r_copies
    for copy in r_copies:
        copy.wait_recv()

    kv_copies = []
    for j in range(4):
        if j == 2:
            relay(3)

        @pl.when(mz > 0)
        def _():
            part_copy(j, 0, mz).wait_recv()

        @pl.when(mz < 3)
        def _():
            part_copy(j, 1, mz).wait_recv()

        block = order[j]
        here = pl.ds(pl.multiple_of(block * rows, rows), rows)
        scale_rows = rms[block]
        cosine, sine = cos_ref[here, :], sin_ref[here, :]
        for at in range(0, 384, 128):
            cols = slice(at, at + 128)
            value = (
                part[j, mz, :, cols].astype(f32)
                + part_in[j, 0, mz, :, cols].astype(f32)
                + part_in[j, 1, mz, :, cols].astype(f32)
            ) * scale_rows
            turned = value * cosine + pltpu.roll(value, 64, 1) * sine
            if at < 256:
                qs[at // 128, here, :] = turned.astype(bf16)
            else:
                kvs[parity, here, :] = jnp.where(parity == 0, turned, value).astype(bf16)
        kv_copies.append(send(
            kvs.at[parity, here], kvs.at[parity, here], k_s.at[j], k_r.at[j],
            {"gx": mz + 1 - 2 * parity},
        ))
    for copy in kv_copies:
        copy.wait_recv()
    sent += kv_copies

    length = kvs.shape[1]
    scale = 1.0 / (HEAD_DIM ** 0.5)
    back = [3, 2, 1, 0]

    def att_copy(j, side, source):
        return pltpu.make_async_remote_copy(
            src_ref=att.at[j, source], dst_ref=att.at[j, source],
            send_sem=a_s.at[j, side, source], recv_sem=a_r.at[j, source],
            device_id=sides[side], device_id_type=pl.DeviceIdType.MESH,
        )

    def attend(j):
        block = order[j]
        here = pl.ds(pl.multiple_of(block * rows, rows), rows)
        index_q = block * rows + lax.broadcasted_iota(jnp.int32, (rows, length), 0)
        index_k = lax.broadcasted_iota(jnp.int32, (rows, length), 1)
        allowed = (idc_ref[here, 0:1] == ids_row) & (index_k <= index_q)
        for h in range(2):
            scores = lax.dot_general(
                qs[h, here, :], kvs[0], (((1,), (1,)), ((), ())), preferred_element_type=f32
            ) * scale
            weights = jnp.where(allowed, jnp.exp(scores), 0.0)
            top = jnp.dot(weights.astype(bf16), kvs[1], preferred_element_type=f32)
            below = jnp.sum(weights, axis=1, keepdims=True)
            att[j, mz, :, h * 128 : h * 128 + 128] = (top / below).astype(bf16)

        @pl.when(mz < 3)
        def _():
            att_copy(j, 0, mz).start()

        @pl.when(mz > 0)
        def _():
            att_copy(j, 1, mz).start()

    def pass_on(j):
        for source in (1, 2, 0, 3):
            @pl.when(mz != source)
            def _():
                att_copy(j, 0, source).wait_recv()

            if source < 2:
                @pl.when((mz > source) & (mz < 3))
                def _():
                    att_copy(j, 0, source).start()
            else:
                @pl.when((mz > 0) & (mz < source))
                def _():
                    att_copy(j, 1, source).start()

    attend(3)
    attend(2)
    o_copies = {}
    loads[3].wait()
    wide_out = wo_ref.shape[1]
    tile = 512
    for n, j in enumerate(back):
        pass_on(j)
        if j > 1:
            attend(j - 2)
        if j == 2:
            o_copies[3].wait_recv()
        if j == 0:
            o_copies[2].wait_recv()
            o_copies[1].wait_recv()

        @pl.loop(0, wide_out // tile)
        def _(i):
            cols = pl.ds(pl.multiple_of(i * tile, tile), tile)
            value = jnp.dot(att[j, 0], wo_ref[0:256, cols], preferred_element_type=f32)
            for d in range(1, 4):
                value = value + jnp.dot(
                    att[j, d], wo_ref[d * 256 : d * 256 + 256, cols], preferred_element_type=f32
                )
            if j == 2:
                value = value + oin[2, :, cols].astype(f32)
            if j == 0:
                value = value + oin[0, :, cols].astype(f32) + oin[1, :, cols].astype(f32)
                out_ref[:, cols] = value.astype(bf16)
            else:
                osend[j - 1, :, cols] = value.astype(bf16)

        if j > 0:
            o_copies[j] = send(
                osend.at[j - 1], oin.at[j - 1], o_s.at[j - 1], o_r.at[j - 1],
                {"gy": across if j == 2 else core},
            )
            sent.append(o_copies[j])
    for copy in sent:
        copy.wait_send()
    for j in range(4):
        for d in range(4):
            if d > 0:
                @pl.when(mz < d)
                def _():
                    part_copy(j, 0, d).wait_send()
            if d < 3:
                @pl.when(mz > d)
                def _():
                    part_copy(j, 1, d).wait_send()

            @pl.when((mz >= d) & (mz < 3))
            def _():
                att_copy(j, 0, d).wait_send()

            @pl.when((mz <= d) & (mz > 0))
            def _():
                att_copy(j, 1, d).wait_send()


def fused_body(tokens, norm_gain, w_query, w_key, w_value, w_output, sequence_ids):
    length = sequence_ids.shape[0]
    rows, feats = tokens.shape
    bf16, f32 = jnp.bfloat16, jnp.float32
    half = HEAD_DIM // 2
    inverse = rope_base ** (-(jnp.arange(half, dtype=f32) * 2.0) / HEAD_DIM)
    inverse = jnp.concatenate([inverse, inverse])[None, :]
    wide_out = w_output.shape[1]
    dma = pltpu.SemaphoreType.DMA
    return pl.pallas_call(
        fused_kernel,
        out_shape=jax.ShapeDtypeStruct((rows, wide_out), bf16),
        in_specs=[pl.BlockSpec(memory_space=pltpu.VMEM)] * 2
        + [pl.BlockSpec(memory_space=pl.ANY)] * 4
        + [pl.BlockSpec(memory_space=pltpu.VMEM)] * 2,
        out_specs=pl.BlockSpec(memory_space=pltpu.VMEM),
        scratch_shapes=[
            pltpu.VMEM((4, rows, feats), bf16),
            pltpu.VMEM((rows, 128), f32),
            pltpu.VMEM((3, rows, 128), f32),
            pltpu.VMEM((4, rows, 128), f32),
            pltpu.VMEM((4, 4, rows, 384), bf16),
            pltpu.VMEM((4, 2, 4, rows, 384), bf16),
            pltpu.VMEM((2, length, 128), bf16),
            pltpu.VMEM((2, length, 128), bf16),
            pltpu.VMEM((4, 4, rows, 256), bf16),
            pltpu.VMEM((3, rows, wide_out), bf16),
            pltpu.VMEM((3, rows, wide_out), bf16),
            dma((3,)), dma((3,)), dma((3,)), dma((3,)), dma((3,)), dma((3,)),
            dma((4, 2, 4)), dma((4, 2, 4)), dma((4, 2, 4)), dma((4, 4)), dma((3,)), dma((3,)),
            dma((4,)), dma((4,)),
            pltpu.VMEM(w_query.shape, bf16),
            pltpu.VMEM(w_key.shape, bf16),
            pltpu.VMEM(w_value.shape, bf16),
            pltpu.VMEM(w_output.shape, bf16),
            dma((4,)),
            pltpu.VMEM((length, 128), f32),
            pltpu.VMEM((length, 128), f32),
            pltpu.VMEM((length, 128), f32),
        ],
        compiler_params=pltpu.CompilerParams(
            collective_id=0, has_side_effects=True, vmem_limit_bytes=56 * 1024 * 1024
        ),
    )(
        tokens, norm_gain[None, :], w_query, w_key, w_value, w_output,
        inverse, sequence_ids[None, :],
    )


def solution(mesh):
    small = mesh.shape["gx"] == 4 and mesh.shape["gy"] == 4
    return jax.shard_map(
        fused_body if small else body,
        mesh=mesh,
        in_specs=(
            P(("groups", "gy"), "gx"),
            P("gx"),
            P("gx", "gy"),
            P("gx", "gy"),
            P("gx", "gy"),
            P("gy", "gx"),
            P("groups"),
        ),
        out_specs=P(("groups", "gy"), "gx"),
        check_vma=False,
    )
```
